256 devices in a mesh: prow: 16 (over x, z_hi), pcol: 16 (over z_lo, y, core).
Axes of the slice: x: 4, y: 4, z: 8 (z_hi: 4, z_lo: 2; z = z_hi * 2 + z_lo), core: 2. Of those that a mesh axis runs over, the one named last changes fastest.
Arguments:
- separator_inverse: float32 [12288, 12288], P('prow', 'pcol'), may hold values from -6 to 6
- panel: float32 [12288, 2048], P('pcol', 'prow'), may hold values from -0.0546875 to 0.0546875
- block_rows: int32 [16], replicated, may hold values 0 or 1
- pivot_inverse: float32 [2048, 2048], P('prow', 'pcol'), may hold values from -4 to 4
Outputs:
- off_diagonal: float32 [12288, 2048], P('prow', 'pcol')
- child_inverse: float32 [2048, 2048], P('prow', 'pcol')
The draws below stay inside these ranges and needn't reach their ends.
All inputs are finite; a program needn't handle non-finite values.
Results may differ from the reference program's by a relative error of at most 0.000088.
Values sent between devices are 32-bit elements; how exact they have to be, the bound alone decides.
No kernel may reach another device: no remote copies, remote signals or barrier semaphores. Data moves between devices by JAX's collectives and lax.ppermute only.
A program may use at most 128 MiB of HBM per device.

```python
import jax
import jax.numpy as jnp
from jax import lax

BS = 768
NB = 16
CW = 2048
NSEP = 12288


def touch_ends(drawn, key, least, high):
    place = [jax.random.randint(jax.random.fold_in(key, axis), (), 0, length) for axis, length in enumerate(drawn.shape)]
    main_axis = drawn.shape.index(max(drawn.shape))
    neighbour = place[:main_axis] + [(place[main_axis] + 1) % drawn.shape[main_axis]] + place[main_axis + 1:]
    return drawn.at[tuple(place)].set(least).at[tuple(neighbour)].set(high)


def block_levels(rng, extent, split, smallest, top_value):
    level, own = 1.0, jax.random.fold_in(rng, 6)
    for dim, parts in split:
        steps = jnp.exp(jax.random.uniform(jax.random.fold_in(own, dim), (parts,), jnp.float32, smallest / len(split), top_value / len(split)))
        level = level * jnp.repeat(steps, extent[dim] // parts).reshape([-1 if axis == dim else 1 for axis in range(len(extent))])
    return level


def gaussian(key, extent, deviation, most, shards=(), dtype=jnp.bfloat16):
    array = jax.random.normal(key, extent, jnp.float32) * deviation
    if len(shards) > 0:
        array = block_levels(key, extent, shards, -0.22, 0.18) * array
    return jnp.clip(array, min=-most, max=most).astype(dtype)


def setup_inputs(seed: int = 0) -> dict:
    streams_of = jax.random.split(jax.random.key(seed), 5)
    return {
        "separator_inverse": gaussian(streams_of[0], (NSEP, NSEP), 1.0, 6.0, ((0, 16), (1, 16)), jnp.float32),
        "panel": gaussian(streams_of[1], (NSEP, CW), NSEP ** -0.5, 0.0546875, ((0, 16), (1, 16)), jnp.float32),
        "block_rows": touch_ends((jax.random.randint(streams_of[2], (NB,), 0, 4) < 3).astype(jnp.int32), jax.random.fold_in(streams_of[2], 1), 0, 1),
        "pivot_inverse": gaussian(streams_of[3], (CW, CW), 0.5, 4.0, ((0, 16), (1, 16)), jnp.float32),
    }


def reference(separator_inverse, panel, block_rows, pivot_inverse):
    keep = jnp.repeat(block_rows.astype(jnp.float32), BS)
    masked = panel * keep[:, None]
    column_sums = jnp.dot(separator_inverse, masked, precision=lax.Precision.HIGHEST, preferred_element_type=jnp.float32)
    off_diagonal = -(column_sums * keep[:, None])
    gram = jnp.dot(masked.T, off_diagonal, precision=lax.Precision.HIGHEST, preferred_element_type=jnp.float32)
    child_inverse = pivot_inverse - gram
    return off_diagonal, child_inverse
```

```python
import jax
import jax.numpy as jnp
from jax import lax
from jax.sharding import PartitionSpec as P

BS = 768
AXES = ("prow", "pcol")
CHUNKS = 1


def places():
    for x in range(4):
        for zh in range(4):
            for zl in range(2):
                for y in range(4):
                    for core in range(2):
                        yield x, zh, zl, y, core


def index_of(x, zh, zl, y, core):
    return ((x % 4) * 4 + zh % 4) * 16 + (zl % 2) * 8 + (y % 4) * 2 + core % 2


def shift(dx=0, dzh=0, dzl=0, dy=0, dcore=0):
    return [
        (index_of(x, zh, zl, y, c), index_of(x + dx, zh + dzh, zl + dzl, y + dy, c + dcore))
        for x, zh, zl, y, c in places()
    ]


def spot(r, i):
    x, zh = i >> 2, i & 3
    return ((zh & 1) ^ (r >> 3)) * 8 + ((x + zh) % 4) * 2 + (zh >> 1)


def block_at(r, c):
    zl, y, core = c >> 3, (c >> 1) & 3, c & 1
    zh = (zl ^ (r >> 3)) + 2 * core
    return lax.rem(y - zh + 4, 4) * 4 + zh


TO_ROW = [(i * 16 + r, r * 16 + spot(r, i)) for i in range(16) for r in range(16)]


def send(value, pairs):
    return lax.ppermute(value, AXES, pairs)


def ring_gather(value, me, axis):
    out = jnp.zeros((4,) + value.shape, value.dtype)
    out = lax.dynamic_update_index_in_dim(out, value, me, 0)
    for step in (1, -1, 2):
        got = send(value, shift(**{axis: step}))
        out = lax.dynamic_update_index_in_dim(out, got, lax.rem(me - step + 4, 4), 0)
    return out


def ring_scatter(value, me, axis, dim):
    pick = lambda place: lax.dynamic_index_in_dim(value, lax.rem(place + 4, 4), dim, keepdims=False)
    got = [send(pick(me + step), shift(**{axis: step})) for step in (1, -1, 2)]
    return (pick(me) + got[0]) + (got[1] + got[2])


def dot_t(a, b):
    return lax.dot_general(
        a, b, (((1,), (1,)), ((), ())), precision=lax.Precision.HIGH, preferred_element_type=jnp.float32
    )


def local(separator_inverse, panel, block_rows, pivot_inverse):
    r = lax.axis_index("prow")
    c = lax.axis_index("pcol")
    x, zh = r // 4, lax.rem(r, 4)
    zl, y, core = c // 8, lax.rem(c // 2, 4), lax.rem(c, 2)
    first = core == 0
    keep_c = lax.dynamic_index_in_dim(block_rows, c, 0, keepdims=False).astype(jnp.float32)
    keep_r = lax.dynamic_index_in_dim(block_rows, r, 0, keepdims=False).astype(jnp.float32)
    swap = shift(dcore=1)

    panel_t = (panel * keep_c).T
    low, high = panel_t[:64], panel_t[64:]
    mine = jnp.where(first, low, high)
    theirs = jnp.where(first, high, low)
    mine = jnp.concatenate([mine, send(theirs, swap)], axis=1)
    sep = jnp.concatenate([separator_inverse, send(separator_inverse, swap)], axis=1)

    rows = 64 // CHUNKS
    halves = []
    for t in range(CHUNKS):
        part = mine[rows * t : rows * (t + 1)]
        part = ring_gather(part, zh, "dzh")
        part = ring_gather(part, x, "dx")
        sums = dot_t(part.reshape(16 * rows, 2 * BS), sep)
        sums = ring_scatter(sums.reshape(2, 4, 2, rows, BS), y, "dy", 1)
        other = lax.dynamic_index_in_dim(sums, 1 - zl, 0, keepdims=False)
        own = lax.dynamic_index_in_dim(sums, zl, 0, keepdims=False)
        sums = own + send(other, shift(dzl=1))
        halves.append(sums)

    sums = halves[0] if CHUNKS == 1 else jnp.concatenate(halves, axis=1)
    other = lax.dynamic_index_in_dim(sums, 1 - core, 0, keepdims=False)
    own = lax.dynamic_index_in_dim(sums, core, 0, keepdims=False)
    got = send(other, swap)
    kept = keep_r * jnp.where(first, jnp.concatenate([own, got]), jnp.concatenate([got, own]))
    off_diagonal = -kept.T

    piece = send(panel_t, TO_ROW)
    pieces = jnp.stack([piece, send(piece, shift(dzl=1))])
    pieces = jnp.stack([pieces] + [send(pieces, shift(dy=s)) for s in (1, -1, 2)])
    pieces = jnp.stack([pieces, send(pieces, swap)])
    row_panel = jnp.zeros((16, 128, BS), jnp.float32)
    for dc in range(2):
        for dy, step in enumerate((0, 1, -1, 2)):
            for dz in range(2):
                place = (zl ^ dz) * 8 + lax.rem(y - step + 4, 4) * 2 + (core ^ dc)
                row_panel = lax.dynamic_update_index_in_dim(row_panel, pieces[dc, dy, dz], block_at(r, place), 0)

    gram = dot_t(row_panel.reshape(2048, BS), kept).reshape(4, 4, 128, 128)
    gram = ring_scatter(gram, x, "dx", 0)
    gram = ring_scatter(gram, zh, "dzh", 0)
    return off_diagonal, pivot_inverse + gram


def solution(mesh):
    in_specs = (P("prow", "pcol"), P("pcol", "prow"), P(), P("prow", "pcol"))
    out_specs = (P("prow", "pcol"), P("prow", "pcol"))
    return jax.shard_map(local, mesh=mesh, in_specs=in_specs, out_specs=out_specs, check_vma=False)
```

```python
import functools

import jax
import jax.numpy as jnp
from jax import lax
from jax.experimental import pallas as pl
from jax.experimental.pallas import tpu as pltpu
from jax.sharding import PartitionSpec as P

BS = 768
AXES = ("prow", "pcol")
COST = pl.CostEstimate(flops=1000, bytes_accessed=1000, transcendentals=0)


def places():
    for x in range(4):
        for zh in range(4):
            for zl in range(2):
                for y in range(4):
                    for core in range(2):
                        yield x, zh, zl, y, core


def index_of(x, zh, zl, y, core):
    return ((x % 4) * 4 + zh % 4) * 16 + (zl % 2) * 8 + (y % 4) * 2 + core % 2


def shift(dx=0, dzh=0, dzl=0, dy=0, dcore=0):
    return [
        (index_of(x, zh, zl, y, c), index_of(x + dx, zh + dzh, zl + dzl, y + dy, c + dcore))
        for x, zh, zl, y, c in places()
    ]


def spot(r, i):
    x, zh = i >> 2, i & 3
    return ((zh & 1) ^ (r >> 3)) * 8 + ((x + zh) % 4) * 2 + (zh >> 1)


def block_at(r, zl, y, core):
    zh = (zl ^ (r >> 3)) + 2 * core
    return lax.rem(y - zh + 4, 4) * 4 + zh


TO_ROW = [(i * 16 + r, r * 16 + spot(r, i)) for i in range(16) for r in range(16)]


def send(value, pairs):
    return lax.ppermute(value, AXES, pairs)


STEPS = (0, 1, -1, 2)


def ring_gather(value, axis):
    return [value] + [send(value, shift(**{axis: step})) for step in STEPS[1:]]


def ring_scatter(values, axis):
    got = [send(value, shift(**{axis: step})) for step, value in zip(STEPS[1:], values[1:])]
    return (values[0] + got[0]) + (got[1] + got[2])


def split(value):
    high = lax.reduce_precision(value, 8, 7)
    return high.astype(jnp.bfloat16), (value - high).astype(jnp.bfloat16)


def dot_nt(a, b):
    return lax.dot_general(a, b, (((1,), (1,)), ((), ())), preferred_element_type=jnp.float32)


def store_split(high_ref, low_ref, at, value):
    high = value.astype(jnp.bfloat16)
    high_ref[at] = high
    low_ref[at] = (value - high.astype(jnp.float32)).astype(jnp.bfloat16)


def ring_slot(step):
    step = lax.rem(step + 8, 4)
    return jnp.where(step == 3, 2, jnp.where(step == 2, 3, step))


def product_kernel(rows, me_ref, c0, c1, c2, c3, h0, l0, h1, l1, o0, o1, o2, o3, high, low):
    x, zh, y = me_ref[0], me_ref[1], me_ref[2]
    for sx, ref in enumerate((c0, c1, c2, c3)):
        for sz in range(4):
            xs = lax.rem(x - STEPS[sx] + 4, 4)
            zs = lax.rem(zh - STEPS[sz] + 4, 4)
            to = ring_slot(2 * lax.rem(xs, 2) + zs // 2 - y)
            place = (to * 2 + xs // 2) * 2 + lax.rem(zs, 2)
            at = pl.ds(pl.multiple_of(place * rows, rows), rows)
            store_split(high, low, (at, slice(None)), ref[sz * rows : (sz + 1) * rows, :])
    own, other = slice(0, BS), slice(BS, 2 * BS)
    for n in range(0, BS, 256):
        cols = slice(n, n + 256)
        sums = dot_nt(high[:, own], h0[cols, :]) + dot_nt(high[:, other], h1[cols, :])
        sums += dot_nt(low[:, own], h0[cols, :]) + dot_nt(low[:, other], h1[cols, :])
        sums += dot_nt(high[:, own], l0[cols, :]) + dot_nt(high[:, other], l1[cols, :])
        for i, out in enumerate((o0, o1, o2, o3)):
            out[:, cols] = sums[4 * rows * i : 4 * rows * (i + 1)]


def product(me, parts, sep):
    rows = parts[0].shape[0] // 4
    return pl.pallas_call(
        functools.partial(product_kernel, rows),
        out_shape=[jax.ShapeDtypeStruct((4 * rows, BS), jnp.float32)] * 4,
        in_specs=[pl.BlockSpec(memory_space=pltpu.SMEM)] + [pl.BlockSpec(memory_space=pltpu.VMEM)] * 8,
        out_specs=[pl.BlockSpec(memory_space=pltpu.VMEM)] * 4,
        scratch_shapes=[pltpu.VMEM((16 * rows, 2 * BS), jnp.bfloat16)] * 2,
        compiler_params=pltpu.CompilerParams(vmem_limit_bytes=24 << 20),
        cost_estimate=COST,
        name="product",
    )(me, *parts, *sep)


def join_kernel(outs, parts, *refs):
    rows = refs[0].shape[0] // outs
    for i in range(outs):
        for j in range(parts):
            refs[i - outs][rows * j : rows * (j + 1), :] = refs[j][rows * i : rows * (i + 1), :]


def join(parts, outs, riders=(), others=()):
    rows, width = parts[0].shape
    any_spec = pl.BlockSpec(memory_space=pl.ANY)
    vmem = pl.BlockSpec(memory_space=pltpu.VMEM)
    return pl.pallas_call(
        functools.partial(join_kernel, outs, len(parts)),
        out_shape=[jax.ShapeDtypeStruct(rider.shape, rider.dtype) for rider in riders]
        + [jax.ShapeDtypeStruct((len(parts) * rows // outs, width), jnp.float32)] * outs,
        in_specs=[vmem] * len(parts) + [any_spec] * (len(riders) + len(others)),
        out_specs=[any_spec] * len(riders) + [vmem] * outs,
        input_output_aliases={len(parts) + i: i for i in range(len(riders))},
        cost_estimate=COST,
        name="join",
    )(*parts, *riders, *others)


def tie_kernel(*refs):
    pass


def tie(value, *others):
    any_spec = pl.BlockSpec(memory_space=pl.ANY)
    return pl.pallas_call(
        tie_kernel,
        out_shape=jax.ShapeDtypeStruct(value.shape, value.dtype),
        in_specs=[any_spec] * (1 + len(others)),
        out_specs=any_spec,
        input_output_aliases={0: 0},
        cost_estimate=COST,
        name="tie",
    )(value, *others)


def order_kernel(at_ref, a, b, high, low):
    for i in range(8):
        for half, ref in enumerate((a, b)):
            at = pl.ds(pl.multiple_of(at_ref[8 * half + i] * 128, 128), 128)
            store_split(high, low, (at, slice(None)), ref[i])


def order(at, a, b):
    return pl.pallas_call(
        order_kernel,
        out_shape=[jax.ShapeDtypeStruct((16 * 128, BS), jnp.bfloat16)] * 2,
        in_specs=[pl.BlockSpec(memory_space=pltpu.SMEM)] + [pl.BlockSpec(memory_space=pltpu.VMEM)] * 2,
        out_specs=[pl.BlockSpec(memory_space=pltpu.VMEM)] * 2,
        compiler_params=pltpu.CompilerParams(vmem_limit_bytes=24 << 20),
        cost_estimate=COST,
        name="order",
    )(at, a, b)


def gram_kernel(high, low, kept, o0, o1, o2, o3):
    h = kept[...].astype(jnp.bfloat16)
    l = (kept[...] - h.astype(jnp.float32)).astype(jnp.bfloat16)
    for i, out in enumerate((o0, o1, o2, o3)):
        rows = slice(512 * i, 512 * (i + 1))
        out[...] = dot_nt(high[rows, :], h) + dot_nt(low[rows, :], h) + dot_nt(high[rows, :], l)


def gram_parts(high, low, kept):
    return pl.pallas_call(
        gram_kernel,
        out_shape=[jax.ShapeDtypeStruct((512, kept.shape[0]), jnp.float32)] * 4,
        in_specs=[pl.BlockSpec(memory_space=pltpu.VMEM)] * 3,
        out_specs=[pl.BlockSpec(memory_space=pltpu.VMEM)] * 4,
        compiler_params=pltpu.CompilerParams(vmem_limit_bytes=24 << 20),
        cost_estimate=COST,
        name="gram",
    )(high, low, kept)


def local(separator_inverse, panel, block_rows, pivot_inverse):
    r = lax.axis_index("prow")
    c = lax.axis_index("pcol")
    x, zh = r // 4, lax.rem(r, 4)
    zl, y, core = c // 8, lax.rem(c // 2, 4), lax.rem(c, 2)
    first = core == 0
    keep_c = lax.dynamic_index_in_dim(block_rows, c, 0, keepdims=False).astype(jnp.float32)
    keep_r = lax.dynamic_index_in_dim(block_rows, r, 0, keepdims=False).astype(jnp.float32)
    swap = shift(dcore=1)
    me = jnp.stack([x, zh, y]).astype(jnp.int32)

    panel_t = (panel * keep_c).T
    low, high = panel_t[:64], panel_t[64:]
    mine = jnp.where(first, low, high)
    theirs = jnp.where(first, high, low)
    mine = jnp.concatenate([mine, send(theirs, swap)], axis=1)

    low, high = mine[:32], mine[32:]
    piece = send(panel_t, TO_ROW)
    sep_other = send(separator_inverse, swap)
    sep = split(separator_inverse) + split(sep_other)

    part = ring_gather(low, "dzh")
    high, piece, col0 = join(part, 1, (high, piece), [sep_other])
    x0 = ring_gather(col0, "dx")
    part = ring_gather(high, "dzh")
    col1, col2 = join(part, 2, (), x0[1:])
    groups = [[2 * q + c_ for q in range(8)] for c_ in range(2)]
    pieces = lax.all_gather(piece, "pcol", axis_index_groups=groups)
    x1 = ring_gather(col1, "dx")
    out0 = product(me, x0, sep)
    x2 = ring_gather(tie(col2, x1[1], x1[2], out0[0]), "dx")
    out1 = product(me, x1, sep)
    sums = [ring_scatter(out0, "dy"), ring_scatter(out1, "dy")]
    x2[1] = tie(x2[1], *sums)
    out2 = product(me, x2, sep)
    sums.append(ring_scatter(out2, "dy"))
    halves = []
    for part in sums:
        part = part.reshape(2, 2, -1, BS)
        other = lax.dynamic_index_in_dim(part, 1 - zl, 0, keepdims=False)
        own = lax.dynamic_index_in_dim(part, zl, 0, keepdims=False)
        halves.append(own + send(other, shift(dzl=1)))

    at = []
    for dc in range(2):
        for zl_ in range(2):
            for y_ in range(4):
                block = block_at(r, zl_, y_, core ^ dc)
                at.append(ring_slot(block // 4 - x) * 4 + ring_slot(lax.rem(block, 4) - zh))
    pieces = tie(pieces, out2[0])
    row_panel = order(jnp.stack(at).astype(jnp.int32), pieces, send(pieces, swap))

    sums = jnp.concatenate(halves, axis=1)
    other = lax.dynamic_index_in_dim(sums, 1 - core, 0, keepdims=False)
    own = lax.dynamic_index_in_dim(sums, core, 0, keepdims=False)
    got = send(other, swap)
    kept = keep_r * jnp.where(first, jnp.concatenate([own, got]), jnp.concatenate([got, own]))
    off_diagonal = -kept.T

    gram = ring_scatter(gram_parts(*row_panel, kept), "dx").reshape(4, 128, 128)
    gram = ring_scatter([gram[i] for i in range(4)], "dzh")
    return off_diagonal, pivot_inverse + gram


def solution(mesh):
    in_specs = (P("prow", "pcol"), P("pcol", "prow"), P(), P("prow", "pcol"))
    out_specs = (P("prow", "pcol"), P("prow", "pcol"))
    return jax.shard_map(local, mesh=mesh, in_specs=in_specs, out_specs=out_specs, check_vma=False)
```

```python
import functools

import jax
import jax.numpy as jnp
from jax import lax
from jax.experimental import pallas as pl
from jax.experimental.pallas import tpu as pltpu
from jax.sharding import PartitionSpec as P

BS = 768
AXES = ("prow", "pcol")
SIZES = (16, 32, 16)
FROM = (0, 16, 48)
STEPS = (0, 1, -1, 2)
COST = pl.CostEstimate(flops=1000, bytes_accessed=1000, transcendentals=0)
VMEM = pl.BlockSpec(memory_space=pltpu.VMEM)
SMEM = pl.BlockSpec(memory_space=pltpu.SMEM)
ANY = pl.BlockSpec(memory_space=pl.ANY)


def places():
    for x in range(4):
        for zh in range(4):
            for zl in range(2):
                for y in range(4):
                    for core in range(2):
                        yield x, zh, zl, y, core


def index_of(x, zh, zl, y, core):
    return ((x % 4) * 4 + zh % 4) * 16 + (zl % 2) * 8 + (y % 4) * 2 + core % 2


def shift(dx=0, dzh=0, dzl=0, dy=0, dcore=0):
    return [
        (index_of(x, zh, zl, y, c), index_of(x + dx, zh + dzh, zl + dzl, y + dy, c + dcore))
        for x, zh, zl, y, c in places()
    ]


def to_column(p):
    return [
        (k * 16 + 2 * q + h, (2 * q + (k + p) % 2) * 16 + 2 * (k // 2) + h)
        for k in range(16)
        for q in range(8)
        for h in range(2)
    ]


def to_block(p):
    return [
        (j * 16 + 2 * q + h, (2 * q + (h + p) % 2) * 16 + j)
        for j in range(16)
        for q in range(8)
        for h in range(2)
    ]


def send(value, pairs):
    return lax.ppermute(value, AXES, pairs)


def ring_gather(value, axis):
    return [value] + [send(value, shift(**{axis: step})) for step in STEPS[1:]]


def ring_scatter(values, axis):
    got = [send(value, shift(**{axis: step})) for step, value in zip(STEPS[1:], values[1:])]
    return (values[0] + got[0]) + (got[1] + got[2])


def pick(value, at):
    return lax.dynamic_index_in_dim(value, at, 0, keepdims=False)


def split(value):
    high = lax.reduce_precision(value, 8, 7)
    return high.astype(jnp.bfloat16), (value - high).astype(jnp.bfloat16)


def dot_nt(a, b):
    return lax.dot_general(a, b, (((1,), (1,)), ((), ())), preferred_element_type=jnp.float32)


def store_split(high_ref, low_ref, at, value):
    high = value.astype(jnp.bfloat16)
    high_ref[at] = high
    low_ref[at] = (value - high.astype(jnp.float32)).astype(jnp.bfloat16)


def ring_slot(step):
    step = lax.rem(step + 8, 4)
    return jnp.where(step == 3, 2, jnp.where(step == 2, 3, step))


def product_kernel(rows, me_ref, c0, c1, c2, c3, h0, l0, h1, l1, o0, o1, o2, o3, high, low):
    x, zh, y = me_ref[0], me_ref[1], me_ref[2]
    for sx, ref in enumerate((c0, c1, c2, c3)):
        for sz in range(4):
            xs = lax.rem(x - STEPS[sx] + 4, 4)
            zs = lax.rem(zh - STEPS[sz] + 4, 4)
            to = ring_slot(2 * lax.rem(xs, 2) + zs // 2 - y)
            place = (to * 2 + xs // 2) * 2 + lax.rem(zs, 2)
            at = pl.ds(pl.multiple_of(place * rows, rows), rows)
            store_split(high, low, (at, slice(None)), ref[sz * rows : (sz + 1) * rows, :])
    own, other = slice(0, BS), slice(BS, 2 * BS)
    for n in range(0, BS, 256):
        cols = slice(n, n + 256)
        sums = dot_nt(high[:, own], h0[cols, :]) + dot_nt(high[:, other], h1[cols, :])
        sums += dot_nt(low[:, own], h0[cols, :]) + dot_nt(low[:, other], h1[cols, :])
        sums += dot_nt(high[:, own], l0[cols, :]) + dot_nt(high[:, other], l1[cols, :])
        for i, out in enumerate((o0, o1, o2, o3)):
            out[:, cols] = sums[4 * rows * i : 4 * rows * (i + 1)]


def product(me, parts, sep):
    rows = parts[0].shape[0] // 4
    outs = pl.pallas_call(
        functools.partial(product_kernel, rows),
        out_shape=[jax.ShapeDtypeStruct((4 * rows, BS), jnp.float32)] * 4
        + [jax.ShapeDtypeStruct((16 * rows, 2 * BS), jnp.bfloat16)] * 2,
        in_specs=[SMEM] + [VMEM] * 8,
        out_specs=[VMEM] * 6,
        compiler_params=pltpu.CompilerParams(vmem_limit_bytes=20 << 20),
        cost_estimate=COST,
        name="product",
    )(me, *parts, *sep)
    return outs[:4], outs[4:]


def gram_kernel(me_ref, *refs):
    high, low, got, outs, chigh, clow = refs[0:3], refs[3:6], refs[6:18], refs[18:22], refs[22], refs[23]
    core, turn = me_ref[3], me_ref[4] == 1
    for t, rows in enumerate(SIZES):
        for half in range(2):
            a, b = got[4 * t + 2 * half][...], got[4 * t + 2 * half + 1][...]
            start = 64 * (core if half == 0 else 1 - core) + FROM[t]
            at = pl.ds(pl.multiple_of(start, 16), rows)
            store_split(chigh, clow, (at, slice(0, BS)), jnp.where(turn, b, a))
            store_split(chigh, clow, (at, slice(BS, 2 * BS)), jnp.where(turn, a, b))
    for t, rows in enumerate(SIZES):
        sums = dot_nt(high[t][...], chigh[...]) + dot_nt(low[t][...], chigh[...]) + dot_nt(high[t][...], clow[...])
        for i, out in enumerate(outs):
            for e in range(4):
                at = 64 * e + FROM[t]
                out[at : at + rows, :] = sums[(4 * i + e) * rows : (4 * i + e + 1) * rows]


def gram_parts(me, panels, got):
    return pl.pallas_call(
        gram_kernel,
        out_shape=[jax.ShapeDtypeStruct((256, 128), jnp.float32)] * 4,
        in_specs=[SMEM] + [VMEM] * 18,
        out_specs=[VMEM] * 4,
        scratch_shapes=[pltpu.VMEM((128, 2 * BS), jnp.bfloat16)] * 2,
        compiler_params=pltpu.CompilerParams(vmem_limit_bytes=20 << 20),
        cost_estimate=COST,
        name="gram",
    )(me, *[p[0] for p in panels], *[p[1] for p in panels], *got)


def join_kernel(sizes, parts, *refs):
    start = 0
    for rows, out in zip(sizes, refs[len(refs) - len(sizes) :]):
        for j in range(parts):
            out[rows * j : rows * (j + 1), :] = refs[j][start : start + rows, :]
        start += rows


def join(parts, sizes, riders=(), others=()):
    return pl.pallas_call(
        functools.partial(join_kernel, sizes, len(parts)),
        out_shape=[jax.ShapeDtypeStruct(rider.shape, rider.dtype) for rider in riders]
        + [jax.ShapeDtypeStruct((len(parts) * rows, parts[0].shape[1]), jnp.float32) for rows in sizes],
        in_specs=[VMEM] * len(parts) + [ANY] * (len(riders) + len(others)),
        out_specs=[ANY] * len(riders) + [VMEM] * len(sizes),
        input_output_aliases={len(parts) + i: i for i in range(len(riders))},
        cost_estimate=COST,
        name="join",
    )(*parts, *riders, *others)


def tie_kernel(*refs):
    pass


def tie(value, *others):
    return pl.pallas_call(
        tie_kernel,
        out_shape=jax.ShapeDtypeStruct(value.shape, value.dtype),
        in_specs=[ANY] * (1 + len(others)),
        out_specs=ANY,
        input_output_aliases={0: 0},
        cost_estimate=COST,
        name="tie",
    )(value, *others)


def local(separator_inverse, panel, block_rows, pivot_inverse):
    r = lax.axis_index("prow")
    c = lax.axis_index("pcol")
    x, zh = r // 4, lax.rem(r, 4)
    zl, y, core = c // 8, lax.rem(c // 2, 4), lax.rem(c, 2)
    first = core == 0
    keep_c = pick(block_rows, c).astype(jnp.float32)
    keep_r = pick(block_rows, r).astype(jnp.float32)
    swap = shift(dcore=1)
    me = jnp.stack([x, zh, y, core, lax.rem(r + core, 2)]).astype(jnp.int32)

    panel_t = (panel * keep_c).T
    low, high = panel_t[:64], panel_t[64:]
    mine = jnp.where(first, low, high)
    theirs = jnp.where(first, high, low)
    mine = jnp.concatenate([mine, send(theirs, swap)], axis=1)
    sep_other = send(separator_inverse, swap)
    sep = split(separator_inverse) + split(sep_other)

    lead, rest = mine[: SIZES[0]], mine[SIZES[0] :]
    rest, col0 = join(ring_gather(lead, "dzh"), SIZES[:1], [rest])
    x0 = ring_gather(col0, "dx")
    col1, col2 = join(ring_gather(rest, "dzh"), SIZES[1:], [], [*x0[1:], sep_other])
    x1 = ring_gather(col1, "dx")
    out0, panel0 = product(me, x0, sep)
    x2 = ring_gather(tie(col2, x1[1], x1[2], out0[0]), "dx")
    out1, panel1 = product(me, x1, sep)
    sums0 = ring_scatter(out0, "dy")
    x2[1] = tie(x2[1], sums0)
    out2, panel2 = product(me, x2, sep)
    sums = [sums0, ring_scatter(out1, "dy"), ring_scatter(out2, "dy")]

    own, got = [], []
    for part in sums:
        part = part.reshape(2, 2, -1, BS)
        kept = keep_r * (pick(part, zl) + send(pick(part, 1 - zl), shift(dzl=1)))
        own.append(kept)
        there = [send(pick(kept, lax.rem(r + p, 2)), to_column(p)) for p in range(2)]
        got += there + [send(value, swap) for value in there]

    kept = jnp.concatenate(own, axis=1)
    mine, theirs = pick(kept, core), send(pick(kept, 1 - core), swap)
    off_diagonal = -jnp.where(first, jnp.concatenate([mine, theirs]), jnp.concatenate([theirs, mine])).T

    gram = ring_scatter(gram_parts(me, (panel0, panel1, panel2), got), "dy").reshape(2, 2, 64, 128)
    gram = pick(gram, zl) + send(pick(gram, 1 - zl), shift(dzl=1))
    even, odd = [send(pick(gram, lax.rem(core + p, 2)), to_block(p)) for p in range(2)]
    gram = jnp.where(lax.rem(r, 2) == 0, jnp.concatenate([even, odd]), jnp.concatenate([odd, even]))
    return off_diagonal, pivot_inverse + gram


def solution(mesh):
    in_specs = (P("prow", "pcol"), P("pcol", "prow"), P(), P("prow", "pcol"))
    out_specs = (P("prow", "pcol"), P("prow", "pcol"))
    return jax.shard_map(local, mesh=mesh, in_specs=in_specs, out_specs=out_specs, check_vma=False)
```

```python
import functools

import jax
import jax.numpy as jnp
from jax import lax
from jax.experimental import pallas as pl
from jax.experimental.pallas import tpu as pltpu
from jax.sharding import PartitionSpec as P

BS = 768
AXES = ("prow", "pcol")
SIZES = (16, 32, 16)
FROM = (0, 16, 48)
STEPS = (0, 1, -1, 2)
COST = pl.CostEstimate(flops=1000, bytes_accessed=1000, transcendentals=0)
VMEM = pl.BlockSpec(memory_space=pltpu.VMEM)
SMEM = pl.BlockSpec(memory_space=pltpu.SMEM)
ANY = pl.BlockSpec(memory_space=pl.ANY)


def places():
    for x in range(4):
        for zh in range(4):
            for zl in range(2):
                for y in range(4):
                    for core in range(2):
                        yield x, zh, zl, y, core


def index_of(x, zh, zl, y, core):
    return ((x % 4) * 4 + zh % 4) * 16 + (zl % 2) * 8 + (y % 4) * 2 + core % 2


def shift(dx=0, dzh=0, dzl=0, dy=0, dcore=0):
    return [
        (index_of(x, zh, zl, y, c), index_of(x + dx, zh + dzh, zl + dzl, y + dy, c + dcore))
        for x, zh, zl, y, c in places()
    ]


def row_of(j):
    j0, j1, j2, j3 = j & 1, (j >> 1) & 1, (j >> 2) & 1, j >> 3
    return j3 + 2 * (j0 ^ j1) + 4 * j1 + 8 * (j2 ^ j0)


TO_COLUMN = [(k * 16 + j, row_of(j) * 16 + k) for k in range(16) for j in range(16)]
TO_PLACE = [(row_of(j) * 16 + i, i * 16 + j) for i in range(16) for j in range(16)]


def send(value, pairs):
    return lax.ppermute(value, AXES, pairs)


def ring_gather(value, axis):
    return [value] + [send(value, shift(**{axis: step})) for step in STEPS[1:]]


def ring_forward(value, axis):
    half = value.shape[0] // 2
    up, down = (send(value, shift(**{axis: step})) for step in STEPS[1:3])
    far = [send(up[:half], shift(**{axis: 1})), send(down[half:], shift(**{axis: -1}))]
    return [value, up, down, *far]


def ring_scatter(values, axis):
    got = [send(value, shift(**{axis: step})) for step, value in zip(STEPS[1:], values[1:])]
    return (values[0] + got[0]) + (got[1] + got[2])


def pick(value, at):
    return lax.dynamic_index_in_dim(value, at, 0, keepdims=False)


def split(value):
    high = lax.reduce_precision(value, 8, 7)
    return high.astype(jnp.bfloat16), (value - high).astype(jnp.bfloat16)


def dot_nt(a, b):
    return lax.dot_general(a, b, (((1,), (1,)), ((), ())), preferred_element_type=jnp.float32)


def store_split(high_ref, low_ref, at, value):
    high = value.astype(jnp.bfloat16)
    high_ref[at] = high
    low_ref[at] = (value - high.astype(jnp.float32)).astype(jnp.bfloat16)


def ring_slot(step):
    step = lax.rem(step + 8, 4)
    return jnp.where(step == 3, 2, jnp.where(step == 2, 3, step))


def product_kernel(rows, me_ref, c0, c1, c2, c3, h0, l0, h1, l1, o0, o1, o2, o3, high, low):
    x, zh, y = me_ref[0], me_ref[1], me_ref[2]
    for sx, ref in enumerate((c0, c1, c2, c3)):
        for sz in range(4):
            xs = lax.rem(x - STEPS[sx] + 4, 4)
            zs = lax.rem(zh - STEPS[sz] + 4, 4)
            to = ring_slot(2 * lax.rem(xs, 2) + zs // 2 - y)
            place = (to * 2 + xs // 2) * 2 + lax.rem(zs, 2)
            at = pl.ds(pl.multiple_of(place * rows, rows), rows)
            store_split(high, low, (at, slice(None)), ref[sz * rows : (sz + 1) * rows, :])
    own, other = slice(0, BS), slice(BS, 2 * BS)
    for n in range(0, BS, 256):
        cols = slice(n, n + 256)
        sums = dot_nt(high[:, own], h0[cols, :]) + dot_nt(high[:, other], h1[cols, :])
        sums += dot_nt(low[:, own], h0[cols, :]) + dot_nt(low[:, other], h1[cols, :])
        sums += dot_nt(high[:, own], l0[cols, :]) + dot_nt(high[:, other], l1[cols, :])
        for i, out in enumerate((o0, o1, o2, o3)):
            out[:, cols] = sums[4 * rows * i : 4 * rows * (i + 1)]


def product(me, parts, sep):
    rows = parts[0].shape[0] // 4
    outs = pl.pallas_call(
        functools.partial(product_kernel, rows),
        out_shape=[jax.ShapeDtypeStruct((4 * rows, BS), jnp.float32)] * 4
        + [jax.ShapeDtypeStruct((16 * rows, 2 * BS), jnp.bfloat16)] * 2,
        in_specs=[SMEM] + [VMEM] * 8,
        out_specs=[VMEM] * 6,
        compiler_params=pltpu.CompilerParams(vmem_limit_bytes=18 << 20),
        cost_estimate=COST,
        name="product",
    )(me, *parts, *sep)
    return outs[:4], outs[4:]


def gram_kernel(*refs):
    high, low, own, other, outs, chigh, clow = refs[0:3], refs[3:6], refs[6], refs[7], refs[8:12], refs[12], refs[13]
    store_split(chigh, clow, (slice(None), slice(0, BS)), own[...])
    store_split(chigh, clow, (slice(None), slice(BS, 2 * BS)), other[...])
    for t, rows in enumerate(SIZES):
        sums = dot_nt(high[t][...], chigh[...]) + dot_nt(low[t][...], chigh[...]) + dot_nt(high[t][...], clow[...])
        for i, out in enumerate(outs):
            for e in range(4):
                at = 64 * e + FROM[t]
                out[at : at + rows, :] = sums[(4 * i + e) * rows : (4 * i + e + 1) * rows]


def gram_parts(panels, own, other):
    return pl.pallas_call(
        gram_kernel,
        out_shape=[jax.ShapeDtypeStruct((256, 128), jnp.float32)] * 4,
        in_specs=[VMEM] * 8,
        out_specs=[VMEM] * 4,
        scratch_shapes=[pltpu.VMEM((128, 2 * BS), jnp.bfloat16)] * 2,
        compiler_params=pltpu.CompilerParams(vmem_limit_bytes=14 << 20),
        cost_estimate=COST,
        name="gram",
    )(*[p[0] for p in panels], *[p[1] for p in panels], own, other)


def join_kernel(sizes, parts, *refs):
    values = [ref[...] for ref in refs[: min(parts, 3)]]
    values.append(jnp.concatenate([ref[...] for ref in refs[3:parts]]) if parts > 4 else refs[3][...])
    start = 0
    for rows, out in zip(sizes, refs[len(refs) - len(sizes) :]):
        for j, value in enumerate(values):
            out[rows * j : rows * (j + 1), :] = value[start : start + rows]
        start += rows


def join(parts, sizes, riders=(), others=()):
    return pl.pallas_call(
        functools.partial(join_kernel, sizes, len(parts)),
        out_shape=[jax.ShapeDtypeStruct(rider.shape, rider.dtype) for rider in riders]
        + [jax.ShapeDtypeStruct((4 * rows, parts[0].shape[1]), jnp.float32) for rows in sizes],
        in_specs=[VMEM] * len(parts) + [ANY] * (len(riders) + len(others)),
        out_specs=[ANY] * len(riders) + [VMEM] * len(sizes),
        input_output_aliases={len(parts) + i: i for i in range(len(riders))},
        compiler_params=pltpu.CompilerParams(vmem_limit_bytes=4 << 20),
        cost_estimate=COST,
        name="join",
    )(*parts, *riders, *others)


def tie_kernel(*refs):
    pass


def tie(value, *others):
    return pl.pallas_call(
        tie_kernel,
        out_shape=jax.ShapeDtypeStruct(value.shape, value.dtype),
        in_specs=[ANY] * (1 + len(others)),
        out_specs=ANY,
        input_output_aliases={0: 0},
        compiler_params=pltpu.CompilerParams(vmem_limit_bytes=1 << 20),
        cost_estimate=COST,
        name="tie",
    )(value, *others)


def local(separator_inverse, panel, block_rows, pivot_inverse):
    r = lax.axis_index("prow")
    c = lax.axis_index("pcol")
    x, zh = r // 4, lax.rem(r, 4)
    zl, y, core = c // 8, lax.rem(c // 2, 4), lax.rem(c, 2)
    first = core == 0
    keep_c = pick(block_rows, c).astype(jnp.float32)
    keep_r = pick(block_rows, r).astype(jnp.float32)
    swap = shift(dcore=1)
    me = jnp.stack([x, zh, y]).astype(jnp.int32)

    def from_chips(part):
        part = part.reshape(2, 2, -1, BS)
        return keep_r * (pick(part, zl) + send(pick(part, 1 - zl), shift(dzl=1)))

    panel_t = (panel * keep_c).T
    low, high = panel_t[:64], panel_t[64:]
    mine = jnp.where(first, low, high)
    theirs = jnp.where(first, high, low)
    mine = jnp.concatenate([mine, send(theirs, swap)], axis=1)
    sep_other = send(separator_inverse, swap)
    sep = split(separator_inverse) + split(sep_other)

    lead, rest = mine[: SIZES[0]], mine[SIZES[0] :]
    rest, col0 = join(ring_gather(lead, "dzh"), SIZES[:1], [rest])
    x0 = ring_gather(col0, "dx")
    x0[0], col1, col2 = join(ring_forward(rest, "dzh"), SIZES[1:], [col0], [*x0[1:], *sep[2:]])
    x1 = ring_gather(col1, "dx")
    out0, panel0 = product(me, x0, sep)
    own = [from_chips(ring_scatter(out0, "dy"))]
    x2 = ring_gather(tie(col2, *x1[1:], own[0]), "dx")
    out1, panel1 = product(me, x1, sep)
    sums1 = ring_scatter(out1, "dy")
    out2, panel2 = product(me, x2, sep)
    sums2 = ring_scatter(out2, "dy")
    own += [from_chips(sums1), from_chips(sums2)]

    def whole(value):
        mine, theirs = pick(value, core), send(pick(value, 1 - core), swap)
        return jnp.where(first, jnp.concatenate([mine, theirs]), jnp.concatenate([theirs, mine]))

    kept = whole(jnp.concatenate(own, axis=1))
    column = send(kept, TO_COLUMN)
    gram = gram_parts((panel0, panel1, panel2), column, send(column, swap))
    off_diagonal = -kept.T
    gram = ring_scatter(gram, "dy").reshape(2, 2, 64, 128)
    gram = whole(pick(gram, zl) + send(pick(gram, 1 - zl), shift(dzl=1)))
    gram = send(gram, TO_PLACE)
    return off_diagonal, pivot_inverse + gram


def solution(mesh):
    in_specs = (P("prow", "pcol"), P("pcol", "prow"), P(), P("prow", "pcol"))
    out_specs = (P("prow", "pcol"), P("prow", "pcol"))
    return jax.shard_map(local, mesh=mesh, in_specs=in_specs, out_specs=out_specs, check_vma=False)
```

```python
import functools

import jax
import jax.numpy as jnp
from jax import lax
from jax.experimental import pallas as pl
from jax.experimental.pallas import tpu as pltpu
from jax.sharding import PartitionSpec as P

BS = 768
AXES = ("prow", "pcol")
SIZES = (32, 32)
FROM = (0, 32)
STEPS = (0, 1, -1, 2)
COST = pl.CostEstimate(flops=1000, bytes_accessed=1000, transcendentals=0)
VMEM = pl.BlockSpec(memory_space=pltpu.VMEM)
SMEM = pl.BlockSpec(memory_space=pltpu.SMEM)
ANY = pl.BlockSpec(memory_space=pl.ANY)
HBM = pl.BlockSpec(memory_space=pltpu.HBM)


def places():
    for x in range(4):
        for zh in range(4):
            for zl in range(2):
                for y in range(4):
                    for core in range(2):
                        yield x, zh, zl, y, core


def index_of(x, zh, zl, y, core):
    return ((x % 4) * 4 + zh % 4) * 16 + (zl % 2) * 8 + (y % 4) * 2 + core % 2


def shift(dx=0, dzh=0, dzl=0, dy=0, dcore=0):
    return [
        (index_of(x, zh, zl, y, c), index_of(x + dx, zh + dzh, zl + dzl, y + dy, c + dcore))
        for x, zh, zl, y, c in places()
    ]


def row_of(j):
    j0, j1, j2, j3 = j & 1, (j >> 1) & 1, (j >> 2) & 1, j >> 3
    return j3 + 2 * (j0 ^ j1) + 4 * j1 + 8 * (j2 ^ j0)


TO_COLUMN = [(k * 16 + j, row_of(j) * 16 + k) for k in range(16) for j in range(16)]
TO_PLACE = [(row_of(j) * 16 + i, i * 16 + j) for i in range(16) for j in range(16)]


def send(value, pairs):
    return lax.ppermute(value, AXES, pairs)


def ring_gather(value, axis):
    return [value] + [send(value, shift(**{axis: step})) for step in STEPS[1:]]


def ring_forward(value, axis):
    half = value.shape[0] // 2
    up, down = (send(value, shift(**{axis: step})) for step in STEPS[1:3])
    far = [send(up[:half], shift(**{axis: 1})), send(down[half:], shift(**{axis: -1}))]
    return [value, up, down, *far]


def ring_scatter(values, axis):
    got = [send(value, shift(**{axis: step})) for step, value in zip(STEPS[1:], values[1:])]
    return (values[0] + got[0]) + (got[1] + got[2])


def pick(value, at):
    return lax.dynamic_index_in_dim(value, at, 0, keepdims=False)


def split(value):
    high = lax.reduce_precision(value, 8, 7)
    return high.astype(jnp.bfloat16), (value - high).astype(jnp.bfloat16)


def dot_nt(a, b):
    return lax.dot_general(a, b, (((1,), (1,)), ((), ())), preferred_element_type=jnp.float32)


def store_split(high_ref, low_ref, at, value):
    high = value.astype(jnp.bfloat16)
    high_ref[at] = high
    low_ref[at] = (value - high.astype(jnp.float32)).astype(jnp.bfloat16)


def ring_slot(step):
    step = lax.rem(step + 8, 4)
    return jnp.where(step == 3, 2, jnp.where(step == 2, 3, step))


def product_kernel(rows, me_ref, c0, c1, c2, c3, h0, l0, h1, l1, *refs):
    outs, high_out, low_out, high, low, sep, sems = refs[:4], refs[4], refs[5], refs[6], refs[7], refs[8:12], refs[12]
    loads = [pltpu.make_async_copy(src, dst, sems.at[i]) for i, (src, dst) in enumerate(zip((h0, l0, h1, l1), sep))]
    for load in loads:
        load.start()
    x, zh, y = me_ref[0], me_ref[1], me_ref[2]
    for sx, ref in enumerate((c0, c1, c2, c3)):
        for sz in range(4):
            xs = lax.rem(x - STEPS[sx] + 4, 4)
            zs = lax.rem(zh - STEPS[sz] + 4, 4)
            to = ring_slot(2 * lax.rem(xs, 2) + zs // 2 - y)
            place = (to * 2 + xs // 2) * 2 + lax.rem(zs, 2)
            at = pl.ds(pl.multiple_of(place * rows, rows), rows)
            store_split(high, low, (at, slice(None)), ref[sz * rows : (sz + 1) * rows, :])
    stores = [pltpu.make_async_copy(high, high_out, sems.at[4]), pltpu.make_async_copy(low, low_out, sems.at[5])]
    for store in stores:
        store.start()
    for load in loads:
        load.wait()
    h0, l0, h1, l1 = sep
    own, other = slice(0, BS), slice(BS, 2 * BS)
    for n in range(0, BS, 256):
        cols = slice(n, n + 256)
        sums = dot_nt(high[:, own], h0[cols, :]) + dot_nt(high[:, other], h1[cols, :])
        sums += dot_nt(low[:, own], h0[cols, :]) + dot_nt(low[:, other], h1[cols, :])
        sums += dot_nt(high[:, own], l0[cols, :]) + dot_nt(high[:, other], l1[cols, :])
        for i, out in enumerate(outs):
            out[:, cols] = sums[4 * rows * i : 4 * rows * (i + 1)]
    for store in stores:
        store.wait()


def product(me, parts, sep):
    rows = parts[0].shape[0] // 4
    outs = pl.pallas_call(
        functools.partial(product_kernel, rows),
        out_shape=[jax.ShapeDtypeStruct((4 * rows, BS), jnp.float32)] * 4
        + [jax.ShapeDtypeStruct((16 * rows, 2 * BS), jnp.bfloat16)] * 2,
        in_specs=[SMEM] + [VMEM] * 4 + [HBM] * 4,
        out_specs=[VMEM] * 4 + [HBM] * 2,
        scratch_shapes=[pltpu.VMEM((16 * rows, 2 * BS), jnp.bfloat16)] * 2
        + [pltpu.VMEM((BS, BS), jnp.bfloat16)] * 4
        + [pltpu.SemaphoreType.DMA((6,))],
        compiler_params=pltpu.CompilerParams(vmem_limit_bytes=18 << 20),
        cost_estimate=COST,
        name="product",
    )(me, *parts, *sep)
    return list(outs[:4]), outs[4:]


def gram_kernel(*refs):
    panels, columns, outs, held, chigh, clow, sems = refs[:4], refs[4:8], refs[8:12], refs[12:16], refs[16], refs[17], refs[18]
    loads = [pltpu.make_async_copy(src, dst, sems.at[i]) for i, (src, dst) in enumerate(zip(panels, held))]
    for load in loads:
        load.start()
    at = 0
    for half in range(2):
        for group, rows in enumerate(SIZES):
            for i in range(2):
                value = columns[2 * group + i][rows * half : rows * (half + 1), :]
                store_split(chigh, clow, (slice(at, at + rows), slice(BS * i, BS * (i + 1))), value)
            at += rows
    for t, rows in enumerate(SIZES):
        loads[2 * t].wait()
        loads[2 * t + 1].wait()
        high, low = held[2 * t][...], held[2 * t + 1][...]
        sums = dot_nt(high, chigh[...]) + dot_nt(low, chigh[...]) + dot_nt(high, clow[...])
        for i, out in enumerate(outs):
            for e in range(4):
                at = 64 * e + FROM[t]
                out[at : at + rows, :] = sums[(4 * i + e) * rows : (4 * i + e + 1) * rows]


def gram_parts(panels, columns):
    return pl.pallas_call(
        gram_kernel,
        out_shape=[jax.ShapeDtypeStruct((256, 128), jnp.float32)] * 4,
        in_specs=[HBM] * 4 + [VMEM] * 4,
        out_specs=[VMEM] * 4,
        scratch_shapes=[pltpu.VMEM((16 * rows, 2 * BS), jnp.bfloat16) for rows in SIZES for i in range(2)]
        + [pltpu.VMEM((128, 2 * BS), jnp.bfloat16)] * 2
        + [pltpu.SemaphoreType.DMA((4,))],
        compiler_params=pltpu.CompilerParams(vmem_limit_bytes=14 << 20),
        cost_estimate=COST,
        name="gram",
    )(*[p for panel in panels for p in panel], *columns)


def join_kernel(sizes, parts, *refs):
    values = [ref[...] for ref in refs[: min(parts, 3)]]
    values.append(jnp.concatenate([ref[...] for ref in refs[3:parts]]) if parts > 4 else refs[3][...])
    start = 0
    for rows, out in zip(sizes, refs[len(refs) - len(sizes) :]):
        for j, value in enumerate(values):
            out[rows * j : rows * (j + 1), :] = value[start : start + rows]
        start += rows


def join(parts, sizes, riders=(), others=()):
    return pl.pallas_call(
        functools.partial(join_kernel, sizes, len(parts)),
        out_shape=[jax.ShapeDtypeStruct(rider.shape, rider.dtype) for rider in riders]
        + [jax.ShapeDtypeStruct((4 * rows, parts[0].shape[1]), jnp.float32) for rows in sizes],
        in_specs=[VMEM] * len(parts) + [ANY] * (len(riders) + len(others)),
        out_specs=[ANY] * len(riders) + [VMEM] * len(sizes),
        input_output_aliases={len(parts) + i: i for i in range(len(riders))},
        compiler_params=pltpu.CompilerParams(vmem_limit_bytes=4 << 20),
        cost_estimate=COST,
        name="join",
    )(*parts, *riders, *others)


def tie_kernel(*refs):
    pass


def tie(value, *others):
    return pl.pallas_call(
        tie_kernel,
        out_shape=jax.ShapeDtypeStruct(value.shape, value.dtype),
        in_specs=[ANY] * (1 + len(others)),
        out_specs=ANY,
        input_output_aliases={0: 0},
        compiler_params=pltpu.CompilerParams(vmem_limit_bytes=1 << 20),
        cost_estimate=COST,
        name="tie",
    )(value, *others)


def local(separator_inverse, panel, block_rows, pivot_inverse):
    r = lax.axis_index("prow")
    c = lax.axis_index("pcol")
    x, zh = r // 4, lax.rem(r, 4)
    zl, y, core = c // 8, lax.rem(c // 2, 4), lax.rem(c, 2)
    first = core == 0
    keep_c = pick(block_rows, c).astype(jnp.float32)
    keep_r = pick(block_rows, r).astype(jnp.float32)
    swap = shift(dcore=1)
    me = jnp.stack([x, zh, y]).astype(jnp.int32)

    def from_chips(part):
        part = part.reshape(2, 2, -1, BS)
        return keep_r * (pick(part, zl) + send(pick(part, 1 - zl), shift(dzl=1)))

    def whole(value):
        mine, theirs = pick(value, core), send(pick(value, 1 - core), swap)
        return jnp.where(first, jnp.concatenate([mine, theirs]), jnp.concatenate([theirs, mine]))

    panel_t = (panel * keep_c).T
    low, high = panel_t[:64], panel_t[64:]
    mine = jnp.where(first, low, high)
    theirs = jnp.where(first, high, low)
    mine = jnp.concatenate([mine, send(theirs, swap)], axis=1)
    sep_other = send(separator_inverse, swap)
    sep = split(separator_inverse) + split(sep_other)

    lead, rest = mine[: SIZES[0]], mine[SIZES[0] :]
    rest, col0 = join(ring_gather(lead, "dzh"), SIZES[:1], [rest])
    x0 = ring_gather(col0, "dx")
    col0, col1 = join(ring_forward(rest, "dzh"), SIZES[1:], [col0], [*x0[1:], *sep])
    x1 = ring_gather(col1, "dx")
    x0[0] = col0
    out0, panel0 = product(me, x0, sep)
    out1, panel1 = product(me, x1, sep)
    out0[0] = tie(out0[0], out1[0])
    kept0 = whole(from_chips(ring_scatter(out0, "dy")))
    column0 = send(kept0, TO_COLUMN)
    out1[0] = tie(out1[0], column0)
    kept1 = whole(from_chips(ring_scatter(out1, "dy")))
    column1 = send(kept1, TO_COLUMN)
    columns = [column0, send(column0, swap), column1, send(column1, swap)]
    gram = gram_parts((panel0, panel1), columns)
    kept = jnp.concatenate([kept0[:32], kept1[:32], kept0[32:], kept1[32:]])
    off_diagonal = -kept.T
    gram = ring_scatter(gram, "dy").reshape(2, 2, 64, 128)
    gram = whole(pick(gram, zl) + send(pick(gram, 1 - zl), shift(dzl=1)))
    gram = send(gram, TO_PLACE)
    return off_diagonal, pivot_inverse + gram


def solution(mesh):
    in_specs = (P("prow", "pcol"), P("pcol", "prow"), P(), P("prow", "pcol"))
    out_specs = (P("prow", "pcol"), P("prow", "pcol"))
    return jax.shard_map(local, mesh=mesh, in_specs=in_specs, out_specs=out_specs, check_vma=False)
```

```python
import functools

import jax
import jax.numpy as jnp
from jax import lax
from jax.experimental import pallas as pl
from jax.experimental.pallas import tpu as pltpu
from jax.sharding import PartitionSpec as P

BS = 768
AXES = ("prow", "pcol")
SIZES = (32, 32)
FROM = (0, 32)
STEPS = (0, 1, -1, 2)
COST = pl.CostEstimate(flops=1000, bytes_accessed=1000, transcendentals=0)
VMEM = pl.BlockSpec(memory_space=pltpu.VMEM)
SMEM = pl.BlockSpec(memory_space=pltpu.SMEM)
ANY = pl.BlockSpec(memory_space=pl.ANY)
HBM = pl.BlockSpec(memory_space=pltpu.HBM)


def places():
    for x in range(4):
        for zh in range(4):
            for zl in range(2):
                for y in range(4):
                    for core in range(2):
                        yield x, zh, zl, y, core


def index_of(x, zh, zl, y, core):
    return ((x % 4) * 4 + zh % 4) * 16 + (zl % 2) * 8 + (y % 4) * 2 + core % 2


def shift(dx=0, dzh=0, dzl=0, dy=0, dcore=0):
    return [
        (index_of(x, zh, zl, y, c), index_of(x + dx, zh + dzh, zl + dzl, y + dy, c + dcore))
        for x, zh, zl, y, c in places()
    ]


def row_of(j):
    j0, j1, j2, j3 = j & 1, (j >> 1) & 1, (j >> 2) & 1, j >> 3
    return j3 + 2 * (j0 ^ j1) + 4 * j1 + 8 * (j2 ^ j0)


TO_COLUMN = [(k * 16 + j, row_of(j) * 16 + k) for k in range(16) for j in range(16)]
TO_PLACE = [(row_of(j) * 16 + i, i * 16 + j) for i in range(16) for j in range(16)]


def send(value, pairs):
    return lax.ppermute(value, AXES, pairs)


def ring_gather(value, axis):
    return [value] + [send(value, shift(**{axis: step})) for step in STEPS[1:]]


def ring_forward(value, axis, work=None):
    half = value.shape[0] // 2
    up, down = (send(value, shift(**{axis: step})) for step in STEPS[1:3])
    if work is not None:
        up = tie(up, work())
    far = [send(up[:half], shift(**{axis: 1})), send(down[half:], shift(**{axis: -1}))]
    return [value, up, down, *far]


def ring_scatter(values, axis):
    return ring_sum(values, ring_send(values, axis))


def ring_send(values, axis):
    return [send(value, shift(**{axis: step})) for step, value in zip(STEPS[1:], values[1:])]


def ring_sum(values, got):
    return (values[0] + got[0]) + (got[1] + got[2])


def pick(value, at):
    return lax.dynamic_index_in_dim(value, at, 0, keepdims=False)


def split(value):
    high = lax.reduce_precision(value, 8, 7)
    return high.astype(jnp.bfloat16), (value - high).astype(jnp.bfloat16)


def dot_nt(a, b):
    return lax.dot_general(a, b, (((1,), (1,)), ((), ())), preferred_element_type=jnp.float32)


def store_split(high_ref, low_ref, at, value):
    high = value.astype(jnp.bfloat16)
    high_ref[at] = high
    low_ref[at] = (value - high.astype(jnp.float32)).astype(jnp.bfloat16)


def ring_slot(step):
    step = lax.rem(step + 8, 4)
    return jnp.where(step == 3, 2, jnp.where(step == 2, 3, step))


def product_kernel(rows, me_ref, c0, c1, c2, c3, c4, h0, l0, h1, l1, *refs):
    outs, high_out, low_out, high, low, sep, sems = refs[:4], refs[4], refs[5], refs[6], refs[7], refs[8:12], refs[12]
    loads = [pltpu.make_async_copy(src, dst, sems.at[i]) for i, (src, dst) in enumerate(zip((h0, l0, h1, l1), sep))]
    for load in loads:
        load.start()
    x, zh, y = me_ref[0], me_ref[1], me_ref[2]
    for sx in range(4):
        for sz in range(4):
            ref, start = (c0, c1, c2, c3)[sx], sz * rows
            if sx == 3 and sz >= 2:
                ref, start = c4, start - 2 * rows
            xs = lax.rem(x - STEPS[sx] + 4, 4)
            zs = lax.rem(zh - STEPS[sz] + 4, 4)
            to = ring_slot(2 * lax.rem(xs, 2) + zs // 2 - y)
            place = (to * 2 + xs // 2) * 2 + lax.rem(zs, 2)
            at = pl.ds(pl.multiple_of(place * rows, rows), rows)
            store_split(high, low, (at, slice(None)), ref[start : start + rows, :])
    stores = [pltpu.make_async_copy(high, high_out, sems.at[4]), pltpu.make_async_copy(low, low_out, sems.at[5])]
    for store in stores:
        store.start()
    for load in loads:
        load.wait()
    h0, l0, h1, l1 = sep
    own, other = slice(0, BS), slice(BS, 2 * BS)
    for n in range(0, BS, 256):
        cols = slice(n, n + 256)
        sums = dot_nt(high[:, own], h0[cols, :]) + dot_nt(high[:, other], h1[cols, :])
        sums += dot_nt(low[:, own], h0[cols, :]) + dot_nt(low[:, other], h1[cols, :])
        sums += dot_nt(high[:, own], l0[cols, :]) + dot_nt(high[:, other], l1[cols, :])
        for i, out in enumerate(outs):
            out[:, cols] = sums[4 * rows * i : 4 * rows * (i + 1)]
    for store in stores:
        store.wait()


def product(me, parts, sep):
    rows = parts[0].shape[0] // 4
    outs = pl.pallas_call(
        functools.partial(product_kernel, rows),
        out_shape=[jax.ShapeDtypeStruct((4 * rows, BS), jnp.float32)] * 4
        + [jax.ShapeDtypeStruct((16 * rows, 2 * BS), jnp.bfloat16)] * 2,
        in_specs=[SMEM] + [VMEM] * 5 + [HBM] * 4,
        out_specs=[VMEM] * 4 + [HBM] * 2,
        scratch_shapes=[pltpu.VMEM((16 * rows, 2 * BS), jnp.bfloat16)] * 2
        + [pltpu.VMEM((BS, BS), jnp.bfloat16)] * 4
        + [pltpu.SemaphoreType.DMA((6,))],
        compiler_params=pltpu.CompilerParams(vmem_limit_bytes=18 << 20),
        cost_estimate=COST,
        name="product",
    )(me, *parts, *sep)
    return list(outs[:4]), outs[4:]


def gram_kernel(*refs):
    panels, columns, outs, chigh, clow = refs[:4], refs[4:8], refs[8:12], refs[12], refs[13]
    at = 0
    for half in range(2):
        for group, rows in enumerate(SIZES):
            for i in range(2):
                value = columns[2 * group + i][rows * half : rows * (half + 1), :]
                store_split(chigh, clow, (slice(at, at + rows), slice(BS * i, BS * (i + 1))), value)
            at += rows
    for t, rows in enumerate(SIZES):
        high, low = panels[2 * t][...], panels[2 * t + 1][...]
        sums = dot_nt(high, chigh[...]) + dot_nt(low, chigh[...]) + dot_nt(high, clow[...])
        for i, out in enumerate(outs):
            for e in range(4):
                at = 64 * e + FROM[t]
                out[at : at + rows, :] = sums[(4 * i + e) * rows : (4 * i + e + 1) * rows]


def gram_parts(panels, columns):
    return pl.pallas_call(
        gram_kernel,
        out_shape=[jax.ShapeDtypeStruct((256, 128), jnp.float32)] * 4,
        in_specs=[VMEM] * 8,
        out_specs=[VMEM] * 4,
        scratch_shapes=[pltpu.VMEM((128, 2 * BS), jnp.bfloat16)] * 2,
        compiler_params=pltpu.CompilerParams(vmem_limit_bytes=14 << 20),
        cost_estimate=COST,
        name="gram",
    )(*[p for panel in panels for p in panel], *columns)


def join_kernel(sizes, parts, *refs):
    values = [ref[...] for ref in refs[: min(parts, 3)]]
    values.append(jnp.concatenate([ref[...] for ref in refs[3:parts]]) if parts > 4 else refs[3][...])
    start = 0
    for rows, out in zip(sizes, refs[len(refs) - len(sizes) :]):
        for j, value in enumerate(values):
            out[rows * j : rows * (j + 1), :] = value[start : start + rows]
        start += rows


def join(parts, sizes, riders=(), others=()):
    return pl.pallas_call(
        functools.partial(join_kernel, sizes, len(parts)),
        out_shape=[jax.ShapeDtypeStruct(rider.shape, rider.dtype) for rider in riders]
        + [jax.ShapeDtypeStruct((4 * rows, parts[0].shape[1]), jnp.float32) for rows in sizes],
        in_specs=[VMEM] * len(parts) + [ANY] * (len(riders) + len(others)),
        out_specs=[ANY] * len(riders) + [VMEM] * len(sizes),
        input_output_aliases={len(parts) + i: i for i in range(len(riders))},
        compiler_params=pltpu.CompilerParams(vmem_limit_bytes=4 << 20),
        cost_estimate=COST,
        name="join",
    )(*parts, *riders, *others)


def tie_kernel(*refs):
    pass


def tie(value, *others):
    return pl.pallas_call(
        tie_kernel,
        out_shape=jax.ShapeDtypeStruct(value.shape, value.dtype),
        in_specs=[ANY] * (1 + len(others)),
        out_specs=ANY,
        input_output_aliases={0: 0},
        compiler_params=pltpu.CompilerParams(vmem_limit_bytes=1 << 20),
        cost_estimate=COST,
        name="tie",
    )(value, *others)


def local(separator_inverse, panel, block_rows, pivot_inverse):
    r = lax.axis_index("prow")
    c = lax.axis_index("pcol")
    x, zh = r // 4, lax.rem(r, 4)
    zl, y, core = c // 8, lax.rem(c // 2, 4), lax.rem(c, 2)
    first = core == 0
    keep_c = pick(block_rows, c).astype(jnp.float32)
    keep_r = pick(block_rows, r).astype(jnp.float32)
    swap = shift(dcore=1)
    me = jnp.stack([x, zh, y]).astype(jnp.int32)

    def from_chips(part):
        part = part.reshape(2, 2, -1, BS)
        return keep_r * (pick(part, zl) + send(pick(part, 1 - zl), shift(dzl=1)))

    def whole(value):
        mine, theirs = pick(value, core), send(pick(value, 1 - core), swap)
        return jnp.where(first, jnp.concatenate([mine, theirs]), jnp.concatenate([theirs, mine]))

    panel_t = (panel * keep_c).T
    low, high = panel_t[:64], panel_t[64:]
    mine = jnp.where(first, low, high)
    theirs = jnp.where(first, high, low)
    mine = jnp.concatenate([mine, send(theirs, swap)], axis=1)
    sep_other = send(separator_inverse, swap)
    sep = split(separator_inverse) + split(sep_other)

    lead, rest = mine[: SIZES[0]], mine[SIZES[0] :]
    rest, col0 = join(ring_forward(lead, "dzh"), SIZES[:1], [rest])
    x0 = ring_forward(col0, "dx")
    col0, col1 = join(ring_forward(rest, "dzh"), SIZES[1:], [col0], [*x0[1:], *sep])
    x0[0] = col0
    out0, panel0 = product(me, x0, sep)
    x1 = ring_forward(col1, "dx", lambda: out0[1])
    out1, panel1 = product(me, x1, sep)
    kept0 = whole(from_chips(ring_scatter(out0, "dy")))
    column0 = send(kept0, TO_COLUMN)
    kept1 = whole(from_chips(ring_scatter(out1, "dy")))
    column1 = send(kept1, TO_COLUMN)
    columns = [column0, send(column0, swap), column1, send(column1, swap)]
    gram = gram_parts((panel0, panel1), columns)
    kept = jnp.concatenate([kept0[:32], kept1[:32], kept0[32:], kept1[32:]])
    off_diagonal = -kept.T
    gram = ring_scatter(gram, "dy").reshape(2, 2, 64, 128)
    gram = whole(pick(gram, zl) + send(pick(gram, 1 - zl), shift(dzl=1)))
    gram = send(gram, TO_PLACE)
    return off_diagonal, pivot_inverse + gram


def solution(mesh):
    in_specs = (P("prow", "pcol"), P("pcol", "prow"), P(), P("prow", "pcol"))
    out_specs = (P("prow", "pcol"), P("prow", "pcol"))
    return jax.shard_map(local, mesh=mesh, in_specs=in_specs, out_specs=out_specs, check_vma=False)
```

```python
import functools

import jax
import jax.numpy as jnp
from jax import lax
from jax.experimental import pallas as pl
from jax.experimental.pallas import tpu as pltpu
from jax.sharding import PartitionSpec as P

BS = 768
AXES = ("prow", "pcol")
SIZES = (32, 32)
FROM = (0, 32)
STEPS = (0, 1, -1, 2)
COST = pl.CostEstimate(flops=1000, bytes_accessed=1000, transcendentals=0)
VMEM = pl.BlockSpec(memory_space=pltpu.VMEM)
SMEM = pl.BlockSpec(memory_space=pltpu.SMEM)
ANY = pl.BlockSpec(memory_space=pl.ANY)
HBM = pl.BlockSpec(memory_space=pltpu.HBM)


def places():
    for x in range(4):
        for zh in range(4):
            for zl in range(2):
                for y in range(4):
                    for core in range(2):
                        yield x, zh, zl, y, core


def index_of(x, zh, zl, y, core):
    return ((x % 4) * 4 + zh % 4) * 16 + (zl % 2) * 8 + (y % 4) * 2 + core % 2


def shift(dx=0, dzh=0, dzl=0, dy=0, dcore=0):
    return [
        (index_of(x, zh, zl, y, c), index_of(x + dx, zh + dzh, zl + dzl, y + dy, c + dcore))
        for x, zh, zl, y, c in places()
    ]


def row_of(j):
    j0, j1, j2, j3 = j & 1, (j >> 1) & 1, (j >> 2) & 1, j >> 3
    return j3 + 2 * (j0 ^ j1) + 4 * j1 + 8 * (j2 ^ j0)


TO_COLUMN = [(k * 16 + j, row_of(j) * 16 + k) for k in range(16) for j in range(16)]
TO_PLACE = [(row_of(j) * 16 + i, i * 16 + j) for i in range(16) for j in range(16)]


def send(value, pairs):
    return lax.ppermute(value, AXES, pairs)


def ring_gather(value, axis):
    return [value] + [send(value, shift(**{axis: step})) for step in STEPS[1:]]


def ring_forward(value, axis, work=None):
    half = value.shape[0] // 2
    up, down = (send(value, shift(**{axis: step})) for step in STEPS[1:3])
    if work is not None:
        up = tie(up, work())
    far = [send(up[:half], shift(**{axis: 1})), send(down[half:], shift(**{axis: -1}))]
    return [value, up, down, *far]


def ring_scatter(values, axis):
    return ring_sum(values, ring_send(values, axis))


def ring_send(values, axis):
    return [send(value, shift(**{axis: step})) for step, value in zip(STEPS[1:], values[1:])]


def ring_sum(values, got):
    return (values[0] + got[0]) + (got[1] + got[2])


def pick(value, at):
    return lax.dynamic_index_in_dim(value, at, 0, keepdims=False)


def split(value):
    high = lax.reduce_precision(value, 8, 7)
    return high.astype(jnp.bfloat16), (value - high).astype(jnp.bfloat16)


def dot_nt(a, b):
    return lax.dot_general(a, b, (((1,), (1,)), ((), ())), preferred_element_type=jnp.float32)


def store_split(high_ref, low_ref, at, value):
    high = value.astype(jnp.bfloat16)
    high_ref[at] = high
    low_ref[at] = (value - high.astype(jnp.float32)).astype(jnp.bfloat16)


def ring_slot(step):
    step = lax.rem(step + 8, 4)
    return jnp.where(step == 3, 2, jnp.where(step == 2, 3, step))


def product_kernel(rows, me_ref, *refs):
    parts, sep, outs, high_out, low_out = refs[:5], refs[5:9], refs[9:13], refs[13], refs[14]
    held, matrix, total, high, low, sems = refs[15:20], refs[20:24], refs[24], refs[25], refs[26], refs[27]
    loads = [pltpu.make_async_copy(src, dst, sems.at[i]) for i, (src, dst) in enumerate(zip(parts + sep, held + matrix))]
    for load in loads:
        load.start()
    x, zh, y = me_ref[0], me_ref[1], me_ref[2]
    for sx in range(4):
        loads[sx].wait()
        if sx == 3:
            loads[4].wait()
        for sz in range(4):
            ref, start = held[sx], sz * rows
            if sx == 3 and sz >= 2:
                ref, start = held[4], start - 2 * rows
            xs = lax.rem(x - STEPS[sx] + 4, 4)
            zs = lax.rem(zh - STEPS[sz] + 4, 4)
            to = ring_slot(2 * lax.rem(xs, 2) + zs // 2 - y)
            place = (to * 2 + xs // 2) * 2 + lax.rem(zs, 2)
            at = pl.ds(pl.multiple_of(place * rows, rows), rows)
            store_split(high, low, (at, slice(None)), ref[start : start + rows, :])
    stores = [pltpu.make_async_copy(high, high_out, sems.at[9]), pltpu.make_async_copy(low, low_out, sems.at[10])]
    for store in stores:
        store.start()
    for load in loads[5:]:
        load.wait()
    h0, l0, h1, l1 = matrix
    own, other = slice(0, BS), slice(BS, 2 * BS)
    for n in range(3):
        cols = slice(256 * n, 256 * (n + 1))
        sums = dot_nt(high[:, own], h0[cols, :]) + dot_nt(high[:, other], h1[cols, :])
        sums += dot_nt(low[:, own], h0[cols, :]) + dot_nt(low[:, other], h1[cols, :])
        sums += dot_nt(high[:, own], l0[cols, :]) + dot_nt(high[:, other], l1[cols, :])
        total[:, cols] = sums
        for i, out in enumerate(outs):
            piece = total.at[pl.ds(4 * rows * i, 4 * rows), pl.ds(256 * n, 256)]
            store = pltpu.make_async_copy(piece, out.at[:, pl.ds(256 * n, 256)], sems.at[11 + 4 * n + i])
            store.start()
            stores.append(store)
    for store in stores:
        store.wait()


def product(me, parts, sep):
    rows = parts[0].shape[0] // 4
    outs = pl.pallas_call(
        functools.partial(product_kernel, rows),
        out_shape=[jax.ShapeDtypeStruct((4 * rows, BS), jnp.float32)] * 4
        + [jax.ShapeDtypeStruct((16 * rows, 2 * BS), jnp.bfloat16)] * 2,
        in_specs=[SMEM] + [HBM] * 9,
        out_specs=[HBM] * 6,
        scratch_shapes=[pltpu.VMEM(part.shape, jnp.float32) for part in parts]
        + [pltpu.VMEM((BS, BS), jnp.bfloat16)] * 4
        + [pltpu.VMEM((16 * rows, BS), jnp.float32)]
        + [pltpu.VMEM((16 * rows, 2 * BS), jnp.bfloat16)] * 2
        + [pltpu.SemaphoreType.DMA((23,))],
        compiler_params=pltpu.CompilerParams(vmem_limit_bytes=56 << 20),
        cost_estimate=COST,
        name="product",
    )(me, *parts, *sep)
    return list(outs[:4]), outs[4:]


def gram_kernel(*refs):
    panels, columns, outs, chigh, clow = refs[:4], refs[4:8], refs[8:12], refs[12], refs[13]
    at = 0
    for half in range(2):
        for group, rows in enumerate(SIZES):
            for i in range(2):
                value = columns[2 * group + i][rows * half : rows * (half + 1), :]
                store_split(chigh, clow, (slice(at, at + rows), slice(BS * i, BS * (i + 1))), value)
            at += rows
    for t, rows in enumerate(SIZES):
        high, low = panels[2 * t][...], panels[2 * t + 1][...]
        sums = dot_nt(high, chigh[...]) + dot_nt(low, chigh[...]) + dot_nt(high, clow[...])
        for i, out in enumerate(outs):
            for e in range(4):
                at = 64 * e + FROM[t]
                out[at : at + rows, :] = sums[(4 * i + e) * rows : (4 * i + e + 1) * rows]


def gram_parts(panels, columns):
    return pl.pallas_call(
        gram_kernel,
        out_shape=[jax.ShapeDtypeStruct((256, 128), jnp.float32)] * 4,
        in_specs=[VMEM] * 8,
        out_specs=[VMEM] * 4,
        scratch_shapes=[pltpu.VMEM((128, 2 * BS), jnp.bfloat16)] * 2,
        compiler_params=pltpu.CompilerParams(vmem_limit_bytes=14 << 20),
        cost_estimate=COST,
        name="gram",
    )(*[p for panel in panels for p in panel], *columns)


def join_kernel(sizes, parts, *refs):
    values = [ref[...] for ref in refs[: min(parts, 3)]]
    values.append(jnp.concatenate([ref[...] for ref in refs[3:parts]]) if parts > 4 else refs[3][...])
    start = 0
    for rows, out in zip(sizes, refs[len(refs) - len(sizes) :]):
        for j, value in enumerate(values):
            out[rows * j : rows * (j + 1), :] = value[start : start + rows]
        start += rows


def join(parts, sizes, riders=(), others=()):
    return pl.pallas_call(
        functools.partial(join_kernel, sizes, len(parts)),
        out_shape=[jax.ShapeDtypeStruct(rider.shape, rider.dtype) for rider in riders]
        + [jax.ShapeDtypeStruct((4 * rows, parts[0].shape[1]), jnp.float32) for rows in sizes],
        in_specs=[VMEM] * len(parts) + [ANY] * (len(riders) + len(others)),
        out_specs=[ANY] * len(riders) + [VMEM] * len(sizes),
        input_output_aliases={len(parts) + i: i for i in range(len(riders))},
        compiler_params=pltpu.CompilerParams(vmem_limit_bytes=4 << 20),
        cost_estimate=COST,
        name="join",
    )(*parts, *riders, *others)


def tie_kernel(*refs):
    pass


def tie(value, *others):
    return pl.pallas_call(
        tie_kernel,
        out_shape=jax.ShapeDtypeStruct(value.shape, value.dtype),
        in_specs=[ANY] * (1 + len(others)),
        out_specs=ANY,
        input_output_aliases={0: 0},
        compiler_params=pltpu.CompilerParams(vmem_limit_bytes=1 << 20),
        cost_estimate=COST,
        name="tie",
    )(value, *others)


def local(separator_inverse, panel, block_rows, pivot_inverse):
    r = lax.axis_index("prow")
    c = lax.axis_index("pcol")
    x, zh = r // 4, lax.rem(r, 4)
    zl, y, core = c // 8, lax.rem(c // 2, 4), lax.rem(c, 2)
    first = core == 0
    keep_c = pick(block_rows, c).astype(jnp.float32)
    keep_r = pick(block_rows, r).astype(jnp.float32)
    swap = shift(dcore=1)
    me = jnp.stack([x, zh, y]).astype(jnp.int32)

    def from_chips(part):
        part = part.reshape(2, 2, -1, BS)
        return keep_r * (pick(part, zl) + send(pick(part, 1 - zl), shift(dzl=1)))

    def whole(value):
        mine, theirs = pick(value, core), send(pick(value, 1 - core), swap)
        return jnp.where(first, jnp.concatenate([mine, theirs]), jnp.concatenate([theirs, mine]))

    panel_t = (panel * keep_c).T
    low, high = panel_t[:64], panel_t[64:]
    mine = jnp.where(first, low, high)
    theirs = jnp.where(first, high, low)
    mine = jnp.concatenate([mine, send(theirs, swap)], axis=1)
    sep_other = send(separator_inverse, swap)
    sep = split(separator_inverse) + split(sep_other)

    lead, rest = mine[: SIZES[0]], mine[SIZES[0] :]
    rest, col0 = join(ring_forward(lead, "dzh"), SIZES[:1], [rest])
    x0 = ring_forward(col0, "dx")
    col0, col1 = join(ring_forward(rest, "dzh"), SIZES[1:], [col0], [*x0[1:], *sep])
    x0[0] = col0
    out0, panel0 = product(me, x0, sep)
    x1 = ring_forward(col1, "dx", lambda: out0[1])
    out1, panel1 = product(me, x1, sep)
    kept0 = whole(from_chips(ring_scatter(out0, "dy")))
    column0 = send(kept0, TO_COLUMN)
    kept1 = whole(from_chips(ring_scatter(out1, "dy")))
    column1 = send(kept1, TO_COLUMN)
    columns = [column0, send(column0, swap), column1, send(column1, swap)]
    gram = gram_parts((panel0, panel1), columns)
    kept = jnp.concatenate([kept0[:32], kept1[:32], kept0[32:], kept1[32:]])
    off_diagonal = -kept.T
    gram = ring_scatter(gram, "dy").reshape(2, 2, 64, 128)
    gram = whole(pick(gram, zl) + send(pick(gram, 1 - zl), shift(dzl=1)))
    gram = send(gram, TO_PLACE)
    return off_diagonal, pivot_inverse + gram


def solution(mesh):
    in_specs = (P("prow", "pcol"), P("pcol", "prow"), P(), P("prow", "pcol"))
    out_specs = (P("prow", "pcol"), P("prow", "pcol"))
    return jax.shard_map(local, mesh=mesh, in_specs=in_specs, out_specs=out_specs, check_vma=False)
```

```python
import functools

import jax
import jax.numpy as jnp
from jax import lax
from jax.experimental import pallas as pl
from jax.experimental.pallas import tpu as pltpu
from jax.sharding import PartitionSpec as P

BS = 768
AXES = ("prow", "pcol")
SIZES = (32, 32)
FROM = (0, 32)
STEPS = (0, 1, -1, 2)
COST = pl.CostEstimate(flops=1000, bytes_accessed=1000, transcendentals=0)
VMEM = pl.BlockSpec(memory_space=pltpu.VMEM)
SMEM = pl.BlockSpec(memory_space=pltpu.SMEM)
ANY = pl.BlockSpec(memory_space=pl.ANY)
HBM = pl.BlockSpec(memory_space=pltpu.HBM)


def places():
    for x in range(4):
        for zh in range(4):
            for zl in range(2):
                for y in range(4):
                    for core in range(2):
                        yield x, zh, zl, y, core


def index_of(x, zh, zl, y, core):
    return ((x % 4) * 4 + zh % 4) * 16 + (zl % 2) * 8 + (y % 4) * 2 + core % 2


def shift(dx=0, dzh=0, dzl=0, dy=0, dcore=0):
    return [
        (index_of(x, zh, zl, y, c), index_of(x + dx, zh + dzh, zl + dzl, y + dy, c + dcore))
        for x, zh, zl, y, c in places()
    ]


def row_of(j):
    j0, j1, j2, j3 = j & 1, (j >> 1) & 1, (j >> 2) & 1, j >> 3
    return j3 + 2 * (j0 ^ j1) + 4 * j1 + 8 * (j2 ^ j0)


TO_COLUMN = [(k * 16 + j, row_of(j) * 16 + k) for k in range(16) for j in range(16)]
TO_PLACE = [(row_of(j) * 16 + i, i * 16 + j) for i in range(16) for j in range(16)]


def send(value, pairs):
    return lax.ppermute(value, AXES, pairs)


def ring_gather(value, axis):
    return [value] + [send(value, shift(**{axis: step})) for step in STEPS[1:]]


def ring_forward(value, axis, work=None):
    half = value.shape[0] // 2
    up, down = (send(value, shift(**{axis: step})) for step in STEPS[1:3])
    if work is not None:
        up = tie(up, work())
    far = [send(up[:half], shift(**{axis: 1})), send(down[half:], shift(**{axis: -1}))]
    return [value, up, down, *far]


def ring_scatter(values, axis):
    return ring_sum(values, ring_send(values, axis))


def ring_send(values, axis):
    return [send(value, shift(**{axis: step})) for step, value in zip(STEPS[1:], values[1:])]


def ring_sum(values, got):
    return (values[0] + got[0]) + (got[1] + got[2])


def pick(value, at):
    return lax.dynamic_index_in_dim(value, at, 0, keepdims=False)


def split(value):
    high = lax.reduce_precision(value, 8, 7)
    return high.astype(jnp.bfloat16), (value - high).astype(jnp.bfloat16)


def dot_nt(a, b):
    return lax.dot_general(a, b, (((1,), (1,)), ((), ())), preferred_element_type=jnp.float32)


def store_split(high_ref, low_ref, at, value):
    high = value.astype(jnp.bfloat16)
    high_ref[at] = high
    low_ref[at] = (value - high.astype(jnp.float32)).astype(jnp.bfloat16)


def ring_slot(step):
    step = lax.rem(step + 8, 4)
    return jnp.where(step == 3, 2, jnp.where(step == 2, 3, step))


def product_kernel(rows, me_ref, *refs):
    parts, sep, outs, high_out, low_out = refs[:5], refs[5:9], refs[9:13], refs[13], refs[14]
    held, matrix, total, high, low, sems = refs[15:20], refs[20:24], refs[24], refs[25], refs[26], refs[27]
    loads = [pltpu.make_async_copy(src, dst, sems.at[i]) for i, (src, dst) in enumerate(zip(parts + sep, held + matrix))]
    for load in loads:
        load.start()
    x, zh, y = me_ref[0], me_ref[1], me_ref[2]
    for sx in range(4):
        loads[sx].wait()
        if sx == 3:
            loads[4].wait()
        for sz in range(4):
            ref, start = held[sx], sz * rows
            if sx == 3 and sz >= 2:
                ref, start = held[4], start - 2 * rows
            xs = lax.rem(x - STEPS[sx] + 4, 4)
            zs = lax.rem(zh - STEPS[sz] + 4, 4)
            to = ring_slot(2 * lax.rem(xs, 2) + zs // 2 - y)
            place = (to * 2 + xs // 2) * 2 + lax.rem(zs, 2)
            at = pl.ds(pl.multiple_of(place * rows, rows), rows)
            store_split(high, low, (at, slice(None)), ref[start : start + rows, :])
    stores = [pltpu.make_async_copy(high, high_out, sems.at[9]), pltpu.make_async_copy(low, low_out, sems.at[10])]
    for store in stores:
        store.start()
    for load in loads[5:]:
        load.wait()
    h0, l0, h1, l1 = matrix
    own, other = slice(0, BS), slice(BS, 2 * BS)
    for n in range(3):
        cols = slice(256 * n, 256 * (n + 1))
        sums = dot_nt(high[:, own], h0[cols, :]) + dot_nt(high[:, other], h1[cols, :])
        sums += dot_nt(low[:, own], h0[cols, :]) + dot_nt(low[:, other], h1[cols, :])
        sums += dot_nt(high[:, own], l0[cols, :]) + dot_nt(high[:, other], l1[cols, :])
        total[:, cols] = sums
        for i, out in enumerate(outs):
            piece = total.at[pl.ds(4 * rows * i, 4 * rows), pl.ds(256 * n, 256)]
            store = pltpu.make_async_copy(piece, out.at[:, pl.ds(256 * n, 256)], sems.at[11 + 4 * n + i])
            store.start()
            stores.append(store)
    for store in stores:
        store.wait()


def product(me, parts, sep):
    rows = parts[0].shape[0] // 4
    outs = pl.pallas_call(
        functools.partial(product_kernel, rows),
        out_shape=[jax.ShapeDtypeStruct((4 * rows, BS), jnp.float32)] * 4
        + [jax.ShapeDtypeStruct((16 * rows, 2 * BS), jnp.bfloat16)] * 2,
        in_specs=[SMEM] + [HBM] * 9,
        out_specs=[HBM] * 6,
        scratch_shapes=[pltpu.VMEM(part.shape, jnp.float32) for part in parts]
        + [pltpu.VMEM((BS, BS), jnp.bfloat16)] * 4
        + [pltpu.VMEM((16 * rows, BS), jnp.float32)]
        + [pltpu.VMEM((16 * rows, 2 * BS), jnp.bfloat16)] * 2
        + [pltpu.SemaphoreType.DMA((23,))],
        compiler_params=pltpu.CompilerParams(vmem_limit_bytes=56 << 20),
        cost_estimate=COST,
        name="product",
    )(me, *parts, *sep)
    return list(outs[:4]), outs[4:]


def gram_kernel(*refs):
    panels, columns, outs, chigh, clow = refs[:4], refs[4:8], refs[8:12], refs[12], refs[13]
    at = 0
    for half in range(2):
        for group, rows in enumerate(SIZES):
            for i in range(2):
                value = columns[2 * group + i][rows * half : rows * (half + 1), :]
                store_split(chigh, clow, (slice(at, at + rows), slice(BS * i, BS * (i + 1))), value)
            at += rows
    for t, rows in enumerate(SIZES):
        high, low = panels[2 * t][...], panels[2 * t + 1][...]
        sums = dot_nt(high, chigh[...]) + dot_nt(low, chigh[...]) + dot_nt(high, clow[...])
        for i, out in enumerate(outs):
            for e in range(4):
                at = 64 * e + FROM[t]
                out[at : at + rows, :] = sums[(4 * i + e) * rows : (4 * i + e + 1) * rows]


def gram_parts(panels, columns):
    return pl.pallas_call(
        gram_kernel,
        out_shape=[jax.ShapeDtypeStruct((256, 128), jnp.float32)] * 4,
        in_specs=[VMEM] * 8,
        out_specs=[VMEM] * 4,
        scratch_shapes=[pltpu.VMEM((128, 2 * BS), jnp.bfloat16)] * 2,
        compiler_params=pltpu.CompilerParams(vmem_limit_bytes=14 << 20),
        cost_estimate=COST,
        name="gram",
    )(*[p for panel in panels for p in panel], *columns)


def join_kernel(sizes, parts, *refs):
    values = [ref[...] for ref in refs[: min(parts, 3)]]
    values.append(jnp.concatenate([ref[...] for ref in refs[3:parts]]) if parts > 4 else refs[3][...])
    start = 0
    for rows, out in zip(sizes, refs[len(refs) - len(sizes) :]):
        for j, value in enumerate(values):
            out[rows * j : rows * (j + 1), :] = value[start : start + rows]
        start += rows


def join(parts, sizes, riders=(), others=()):
    return pl.pallas_call(
        functools.partial(join_kernel, sizes, len(parts)),
        out_shape=[jax.ShapeDtypeStruct(rider.shape, rider.dtype) for rider in riders]
        + [jax.ShapeDtypeStruct((4 * rows, parts[0].shape[1]), jnp.float32) for rows in sizes],
        in_specs=[VMEM] * len(parts) + [ANY] * (len(riders) + len(others)),
        out_specs=[ANY] * len(riders) + [VMEM] * len(sizes),
        input_output_aliases={len(parts) + i: i for i in range(len(riders))},
        compiler_params=pltpu.CompilerParams(vmem_limit_bytes=4 << 20),
        cost_estimate=COST,
        name="join",
    )(*parts, *riders, *others)


def tie_kernel(*refs):
    pass


def tie(value, *others):
    return pl.pallas_call(
        tie_kernel,
        out_shape=jax.ShapeDtypeStruct(value.shape, value.dtype),
        in_specs=[ANY] * (1 + len(others)),
        out_specs=ANY,
        input_output_aliases={0: 0},
        compiler_params=pltpu.CompilerParams(vmem_limit_bytes=1 << 20),
        cost_estimate=COST,
        name="tie",
    )(value, *others)


def local(separator_inverse, panel, block_rows, pivot_inverse):
    r = lax.axis_index("prow")
    c = lax.axis_index("pcol")
    x, zh = r // 4, lax.rem(r, 4)
    zl, y, core = c // 8, lax.rem(c // 2, 4), lax.rem(c, 2)
    first = core == 0
    keep_c = pick(block_rows, c).astype(jnp.float32)
    keep_r = pick(block_rows, r).astype(jnp.float32)
    swap = shift(dcore=1)
    me = jnp.stack([x, zh, y]).astype(jnp.int32)

    def from_chips(part):
        part = part.reshape(2, 2, -1, BS)
        return keep_r * (pick(part, zl) + send(pick(part, 1 - zl), shift(dzl=1)))

    def whole(value):
        mine, theirs = pick(value, core), send(pick(value, 1 - core), swap)
        return jnp.where(first, jnp.concatenate([mine, theirs]), jnp.concatenate([theirs, mine]))

    panel_t = (panel * keep_c).T
    low, high = panel_t[:64], panel_t[64:]
    mine = jnp.where(first, low, high)
    theirs = jnp.where(first, high, low)
    mine = jnp.concatenate([mine, send(theirs, swap)], axis=1)
    sep_other = send(separator_inverse, swap)
    sep = split(separator_inverse) + split(sep_other)

    lead, rest = mine[: SIZES[0]], mine[SIZES[0] :]
    rest, col0 = join(ring_forward(lead, "dzh"), SIZES[:1], [rest])
    x0 = ring_forward(col0, "dx")
    col0, col1 = join(ring_forward(rest, "dzh"), SIZES[1:], [col0], [*x0[1:], *sep])
    x0[0] = col0
    out0, panel0 = product(me, x0, sep)
    x1 = ring_forward(col1, "dx", lambda: out0[1])
    out1, panel1 = product(me, x1, sep)
    kept0 = whole(from_chips(ring_scatter(out0, "dy")))
    column0 = send(kept0, TO_COLUMN)
    kept1 = whole(from_chips(ring_scatter(out1, "dy")))
    column1 = send(kept1, TO_COLUMN)
    columns = [column0, send(column0, swap), column1, send(column1, swap)]
    gram = gram_parts((panel0, panel1), columns)
    kept = jnp.concatenate([kept0[:32], kept1[:32], kept0[32:], kept1[32:]])
    off_diagonal = -kept.T
    gram = ring_scatter(gram, "dy").reshape(2, 2, 64, 128)
    block = lambda z, e: lax.dynamic_slice(gram, (z, e, 0, 0), (1, 1, 64, 128)).reshape(64, 128)
    theirs = send(block(1 - zl, 1 - core), shift(dzl=1, dcore=1)) + send(block(zl, 1 - core), swap)
    half = block(zl, core) + send(block(1 - zl, core), shift(dzl=1))
    gram = jnp.where(first, jnp.concatenate([half, theirs]), jnp.concatenate([theirs, half]))
    gram = send(gram, TO_PLACE)
    return off_diagonal, pivot_inverse + gram


def solution(mesh):
    in_specs = (P("prow", "pcol"), P("pcol", "prow"), P(), P("prow", "pcol"))
    out_specs = (P("prow", "pcol"), P("prow", "pcol"))
    return jax.shard_map(local, mesh=mesh, in_specs=in_specs, out_specs=out_specs, check_vma=False)
```
